32 devices in a mesh: group: 8 (over z, y), tp: 4 (over x, core).
Axes of the slice: x: 2, y: 2, z: 4, core: 2. Of those that a mesh axis runs over, the one named last changes fastest.
Arguments:
- pf_query: bfloat16 [2048, 8192], P('group', 'tp'), may hold values from -16 to 16
- pf_cache: bfloat16 [8, 2, 4096, 1024], P('group', None, 'tp'), may hold values from -16 to 16
- pf_offset: int32 [8], replicated, may hold values from 0 to 3840
- dec_query: bfloat16 [16, 8192], P('group', 'tp'), may hold values from -16 to 16
- dec_cache: bfloat16 [24, 2, 2048, 1024], P('group', None, 'tp'), may hold values from -16 to 16
- slot_owner: int32 [24], replicated, may hold values from 0 to 15, as said below
- slot_len: int32 [24], replicated, may hold values from 1 to 2048
Outputs:
- pf_out: bfloat16 [2048, 8192], P('group', 'tp')
- dec_out: bfloat16 [16, 8192], P('group', 'tp')
The draws below stay inside these ranges and needn't reach their ends.
Inputs may be any that keep to these rules, and one draw needn't show every extreme that they name: `slot_owner`: every decode request owns one or two slots.
All inputs are finite; a program needn't handle non-finite values.
Results may differ from the reference program's by a relative error of at most 0.005.
Values may be sent and summed in bfloat16 or wider, within the bound.
A program may use at most 128 MiB of HBM per device.

```python
import math
import jax
import jax.numpy as jnp
from jax import lax

QH = 64
KVH = 8
HD = 128
CH = 256
LP = 4096
SLOT_POSITIONS = 2048
GROUPS = 8
DECODE_REQUESTS = 16
TOTAL_SLOTS = 24


def query_field(key, rows):
    noise_key, factor_key = jax.random.split(key)
    base = jnp.clip(jax.random.normal(noise_key, (rows, QH, HD), jnp.float32), -5.0, 5.0)
    factor = jnp.exp(jax.random.uniform(factor_key, (rows, QH, 1), jnp.float32, math.log(0.3), math.log(3.0)))
    return (base * factor).reshape(rows, QH * HD).astype(jnp.bfloat16)


def cache_entry_name(key, count, length):
    key_part, value_part = jax.random.split(key)
    dims = (count, 1, length, KVH * HD)
    stored_keys = jnp.clip(jax.random.normal(key_part, dims, jnp.float32), -5.0, 5.0)
    stored_values = jnp.clip(jax.random.normal(value_part, dims, jnp.float32), -5.0, 5.0)
    return jnp.concatenate([stored_keys, stored_values], axis=1).astype(jnp.bfloat16)


def draw_pf_query(key, part):
    return query_field(key, GROUPS * CH)


def draw_pf_cache(key, part):
    return cache_entry_name(key, GROUPS, LP)


def draw_dec_query(key, part):
    return query_field(key, DECODE_REQUESTS)


def draw_dec_cache(key, part):
    return cache_entry_name(key, TOTAL_SLOTS, SLOT_POSITIONS)


def draw_pf_offset(key, part):
    value_random_key, placement_random_key = jax.random.split(key)
    offsets = jax.random.randint(value_random_key, (GROUPS,), 0, LP - CH + 1, dtype=jnp.int32)
    selected_picks = jax.random.randint(placement_random_key, (), 0, GROUPS, dtype=jnp.int32)
    return jnp.where(jnp.arange(GROUPS, dtype=jnp.int32) == selected_picks, LP - CH, offsets).astype(jnp.int32)


def draw_slot_owner(key, part):
    return (jax.random.permutation(key, TOTAL_SLOTS) % DECODE_REQUESTS).astype(jnp.int32)


def draw_slot_len(key, part):
    value_random_key, placement_random_key = jax.random.split(key)
    length_list = jax.random.randint(value_random_key, (TOTAL_SLOTS,), 1, SLOT_POSITIONS + 1, dtype=jnp.int32)
    selected_picks = jax.random.randint(placement_random_key, (), 0, TOTAL_SLOTS, dtype=jnp.int32)
    return jnp.where(jnp.arange(TOTAL_SLOTS, dtype=jnp.int32) == selected_picks, SLOT_POSITIONS, length_list).astype(jnp.int32)


def setup_inputs(seed: int = 0) -> dict:
    seeds = jax.random.split(jax.random.key(seed), 8)
    return {
        "pf_query": draw_pf_query(jax.random.fold_in(seeds[7], 71), 0),
        "pf_cache": draw_pf_cache(jax.random.fold_in(seeds[7], 71), 0),
        "pf_offset": draw_pf_offset(jax.random.fold_in(seeds[7], 71), 0),
        "dec_query": draw_dec_query(jax.random.fold_in(seeds[7], 71), 0),
        "dec_cache": draw_dec_cache(jax.random.fold_in(seeds[7], 71), 0),
        "slot_owner": draw_slot_owner(jax.random.fold_in(seeds[7], 71), 0),
        "slot_len": draw_slot_len(jax.random.fold_in(seeds[7], 71), 0),
    }


negative_big = -1.0e30


def rounded_weights(scores, visible):
    maxima = jnp.max(jnp.where(visible, scores, negative_big), axis=-1)
    raw = jnp.where(visible, jnp.exp(jnp.where(visible, scores, negative_big) - maxima[..., None]), 0.0)
    weights = lax.optimization_barrier(raw.astype(jnp.bfloat16)).astype(jnp.float32)
    return maxima, weights


def prefill_group(items):
    queries, cache, offset = items
    rows = queries.shape[0]
    width = QH // KVH
    grouped = jnp.moveaxis(queries.astype(jnp.float32).reshape(rows, KVH, width, HD), 1, 0)
    cache_keys = jnp.moveaxis(cache[0].astype(jnp.float32).reshape(LP, KVH, HD), 1, 0)
    cache_values = jnp.moveaxis(cache[1].astype(jnp.float32).reshape(LP, KVH, HD), 1, 0)
    positions = jnp.arange(LP, dtype=jnp.int32)
    visible = positions[None, :] <= (offset + jnp.arange(rows, dtype=jnp.int32))[:, None]

    def one_head(parts):
        scores = jnp.einsum("qgd,nd->gqn", parts[0], parts[1], precision=lax.Precision.HIGHEST) * (HD ** -0.5)
        maxima, weights = rounded_weights(scores, visible[None])
        totals = jnp.sum(weights, axis=-1)
        weighted = jnp.einsum("gqn,nd->gqd", weights, parts[2], precision=lax.Precision.HIGHEST)
        return weighted / totals[..., None]

    result = lax.map(one_head, (grouped, cache_keys, cache_values))
    result = jnp.moveaxis(result.reshape(QH, rows, HD), 1, 0)
    return result.reshape(rows, QH * HD).astype(jnp.bfloat16)


def decode_slot(items):
    query, cache, length = items
    width = QH // KVH
    grouped = query.astype(jnp.float32).reshape(KVH, width, HD)
    cache_keys = cache[0].astype(jnp.float32).reshape(SLOT_POSITIONS, KVH, HD)
    cache_values = cache[1].astype(jnp.float32).reshape(SLOT_POSITIONS, KVH, HD)
    scores = jnp.einsum("kgd,lkd->kgl", grouped, cache_keys, precision=lax.Precision.HIGHEST) * (HD ** -0.5)
    visible = (jnp.arange(SLOT_POSITIONS, dtype=jnp.int32) < length)[None, None, :]
    maxima, weights = rounded_weights(scores, visible)
    totals = jnp.sum(weights, axis=-1)
    weighted = jnp.einsum("kgl,lkd->kgd", weights, cache_values, precision=lax.Precision.HIGHEST)
    return maxima.reshape(QH), totals.reshape(QH), weighted.reshape(QH, HD)


def reference(pf_query, pf_cache, pf_offset, dec_query, dec_cache, slot_owner, slot_len):
    prefill = lax.map(prefill_group, (pf_query.reshape(GROUPS, CH, QH * HD), pf_cache, pf_offset))
    pf_out = prefill.reshape(GROUPS * CH, QH * HD)
    slot_queries = jnp.take(dec_query, slot_owner, axis=0)
    maxima, totals, weighted = lax.map(decode_slot, (slot_queries, dec_cache, slot_len))
    hits = slot_owner[None, :] == jnp.arange(DECODE_REQUESTS, dtype=jnp.int32)[:, None]
    selected_picks = jnp.where(hits[:, :, None], maxima[None], negative_big)
    largest = jnp.max(selected_picks, axis=1)
    factor = jnp.where(hits[:, :, None], jnp.exp(selected_picks - largest[:, None]), 0.0)
    denominator = jnp.einsum("abh,bh->ah", factor, totals, precision=lax.Precision.HIGHEST)
    numerator = jnp.einsum("abh,bhd->ahd", factor, weighted, precision=lax.Precision.HIGHEST)
    dec_out = (numerator / denominator[..., None]).reshape(DECODE_REQUESTS, QH * HD).astype(jnp.bfloat16)
    return pf_out, dec_out
```

```python
import functools
import math
import jax
import jax.numpy as jnp
from jax import lax
from jax.experimental import pallas as pl
from jax.experimental.pallas import tpu as pltpu
from jax.sharding import PartitionSpec as P

QH = 64
KVH = 8
HD = 128
WIDTH = QH // KVH
LOW = -1e30
SCALE = HD ** (-0.5) * math.log2(math.e)
DIMS_NT = (((1,), (1,)), ((), ()))


def kernel(cfg, off_ref, own_ref, len_ref, q_hbm, kv_hbm, dq_hbm, dkv_hbm, out_ref, dout_ref,
           q_ref, kvbuf, dkv, bias, acc, mrow, dqbuf, dpart, dpeer, dall,
           loc_sem, own_sem, kv_send, kv_recv, dq1_send, dq1_recv, dq2_send, dq2_recv,
           dp_send, dp_recv, da_send, da_recv):
    tp, groups, rows, llen, block, lh, kvl, served, slots, slen = cfg
    pieces = llen // block
    chips = tp // 2
    cols = kvl * HD
    t = lax.axis_index("tp")
    g = lax.axis_index("group")
    chip, core = t // 2, t % 2

    def source(s):
        return lax.rem(chip + s // 2, chips) * 2 + lax.rem(core + s % 2, 2)

    def target(s):
        return lax.rem(chip + chips - s // 2, chips) * 2 + lax.rem(core + s % 2, 2)

    def kv_copy(s, piece):
        dest = target(s)
        col = pl.multiple_of((dest * lh // WIDTH) * HD, HD)
        at = pl.ds(piece * block, block)
        return pltpu.make_async_remote_copy(
            src_ref=kv_hbm.at[0, :, at, pl.ds(col, cols)],
            dst_ref=kvbuf.at[s, :, at, :],
            send_sem=kv_send.at[s, piece],
            recv_sem=kv_recv.at[s, piece],
            device_id={"tp": dest},
            device_id_type=pl.DeviceIdType.MESH,
        )

    def own_copy(piece):
        col = pl.multiple_of((t * lh // WIDTH) * HD, HD)
        at = pl.ds(piece * block, block)
        return pltpu.make_async_copy(
            kv_hbm.at[0, :, at, pl.ds(col, cols)], kvbuf.at[0, :, at, :], own_sem.at[piece])

    def dq1_copy(i):
        return pltpu.make_async_remote_copy(
            src_ref=dq_hbm, dst_ref=dqbuf.at[g, :, t], send_sem=dq1_send.at[i],
            recv_sem=dq1_recv.at[i], device_id={"tp": lax.rem(t + i, tp)},
            device_id_type=pl.DeviceIdType.MESH)

    def dq2_copy(i):
        return pltpu.make_async_remote_copy(
            src_ref=dqbuf.at[g], dst_ref=dqbuf.at[g], send_sem=dq2_send.at[i],
            recv_sem=dq2_recv.at[i], device_id={"group": lax.rem(g + i, groups)},
            device_id_type=pl.DeviceIdType.MESH)

    def dp_copy(i):
        dest = lax.rem(t + i, tp)
        return pltpu.make_async_remote_copy(
            src_ref=dpart.at[dest], dst_ref=dpeer.at[i], send_sem=dp_send.at[i],
            recv_sem=dp_recv.at[i], device_id={"tp": dest},
            device_id_type=pl.DeviceIdType.MESH)

    def da_copy(i):
        return pltpu.make_async_remote_copy(
            src_ref=dall.at[g], dst_ref=dall.at[g], send_sem=da_send.at[i],
            recv_sem=da_recv.at[i], device_id={"group": lax.rem(g + i, groups)},
            device_id_type=pl.DeviceIdType.MESH)

    q_copy = pltpu.make_async_copy(q_hbm, q_ref, loc_sem.at[0])
    dq0_copy = pltpu.make_async_copy(dq_hbm, dqbuf.at[g, :, t], loc_sem.at[1])
    dkv_copy = pltpu.make_async_copy(dkv_hbm, dkv, loc_sem.at[2])
    q_copy.start()
    for p in range(pieces):
        own_copy(p).start()
    dq0_copy.start()

    barrier = pltpu.get_barrier_semaphore()
    for i in range(1, tp):
        pl.semaphore_signal(barrier, inc=1, device_id={"tp": lax.rem(t + i, tp)},
                            device_id_type=pl.DeviceIdType.MESH)
    for i in range(1, groups):
        pl.semaphore_signal(barrier, inc=1, device_id={"group": lax.rem(g + i, groups)},
                            device_id_type=pl.DeviceIdType.MESH)
    acc[...] = jnp.zeros_like(acc)
    mrow[...] = jnp.full_like(mrow, LOW)
    pl.semaphore_wait(barrier, tp - 1 + groups - 1)

    for i in range(1, tp):
        dq1_copy(i).start()
    for j in range(1, chips):
        for p in range(pieces):
            for i in range(2):
                kv_copy(2 * j + i, p).start()
    for p in range(pieces):
        kv_copy(1, p).start()
    dkv_copy.start()

    offset = off_ref[g]

    def attend(s, piece):
        at = pl.ds(piece * block, block)
        base = source(s) * llen + piece * block
        pos = lax.broadcasted_iota(jnp.int32, (rows, block), 1) + base
        tok = lax.broadcasted_iota(jnp.int32, (rows, block), 0) + offset
        bias[...] = jnp.where(pos <= tok, 0.0, LOW)

        def one(h):
            kcol = pl.ds(pl.multiple_of((h // WIDTH) * HD, HD), HD)
            q = q_ref[:, pl.ds(pl.multiple_of(h * HD, HD), HD)]
            k = kvbuf[s, 0, at, kcol]
            v = kvbuf[s, 1, at, kcol]
            sc = lax.dot_general(q, k, DIMS_NT, preferred_element_type=jnp.float32)
            sc = sc * SCALE + bias[...]
            old = mrow[h]
            new = jnp.maximum(old, jnp.max(sc, axis=1, keepdims=True))
            w = jnp.exp2(sc - new[:, :1]).astype(jnp.bfloat16)
            vx = jnp.concatenate([v, jnp.ones_like(v)], axis=1)
            o = jnp.dot(w, vx, preferred_element_type=jnp.float32)
            factor = jnp.exp2(old - new)
            mrow[h] = new
            acc[h] = acc[h] * jnp.concatenate([factor, factor], axis=1) + o

        def pair(b, carry):
            one(2 * b)
            one(2 * b + 1)
            return carry

        lax.fori_loop(0, lh // 2, pair, 0)

    def own_step(p, carry):
        own_copy(p).wait()
        attend(0, p)
        return carry

    def near_step(p, carry):
        kv_copy(1, p).wait_recv()
        attend(1, p)
        return carry

    def far_step(b, carry):
        j = 1 + b // (2 * pieces)
        c = b % (2 * pieces)
        s, p = 2 * j + c % 2, c // 2
        kv_copy(s, p).wait_recv()
        attend(s, p)
        return carry

    q_copy.wait()
    lax.fori_loop(0, pieces, own_step, 0)

    dq0_copy.wait()
    for i in range(1, tp):
        dq1_copy(i).wait_recv()
    for i in range(1, groups):
        dq2_copy(i).start()

    lax.fori_loop(0, pieces, near_step, 0)

    dkv_copy.wait()
    for i in range(1, groups):
        dq2_copy(i).wait_recv()
    for n in range(slots):
        owner = own_ref[g * slots + n]
        query = dqbuf[owner // served, owner % served].reshape(QH, HD)
        wide = jnp.concatenate([query] * KVH, axis=1)
        r = lax.broadcasted_iota(jnp.int32, (QH, KVH * HD), 0) // WIDTH
        c = lax.broadcasted_iota(jnp.int32, (QH, KVH * HD), 1) // HD
        wide = jnp.where(r == c, wide, 0.0).astype(jnp.bfloat16)
        sc = lax.dot_general(wide, dkv[n, 0], DIMS_NT, preferred_element_type=jnp.float32)
        pos = lax.broadcasted_iota(jnp.int32, (QH, slen), 1) + t * slen
        live = pos < len_ref[g * slots + n]
        sc = jnp.where(live, sc * SCALE, LOW)
        top = jnp.max(sc, axis=1, keepdims=True)
        w = jnp.where(live, jnp.exp2(sc - top), 0.0).astype(jnp.bfloat16)
        total = jnp.sum(w.astype(jnp.float32), axis=1, keepdims=True)
        o = jnp.dot(w, dkv[n, 1], preferred_element_type=jnp.float32)
        o = jnp.concatenate(
            [o[k * WIDTH:(k + 1) * WIDTH, k * HD:(k + 1) * HD] for k in range(KVH)], axis=0)
        lane = lax.broadcasted_iota(jnp.int32, (QH, HD), 1)
        stat = jnp.where(lane < HD // 2, top, total)
        for d in range(tp):
            dpart[d, 0, n] = o[d * lh:(d + 1) * lh]
            dpart[d, 1, n] = stat[d * lh:(d + 1) * lh]
    for i in range(1, tp):
        dp_copy(i).start()

    far = 2 * (chips - 1) * pieces
    cut = far // 2
    lax.fori_loop(0, cut, far_step, 0)

    for i in range(1, tp):
        dp_copy(i).wait_recv()
    half = HD // 2
    for n in range(slots):
        accs = [dpart[t, 0, n]] + [dpeer[i, 0, n] for i in range(1, tp)]
        stats = [dpart[t, 1, n]] + [dpeer[i, 1, n] for i in range(1, tp)]
        top = functools.reduce(jnp.maximum, [x[:, :1] for x in stats])
        fac = [jnp.exp2(x[:, :1] - top) for x in stats]
        total = sum(f * x[:, half:half + 1] for f, x in zip(fac, stats))
        lane = lax.broadcasted_iota(jnp.int32, (lh, HD), 1)
        dall[g, 0, n] = sum(f * a for f, a in zip(fac, accs))
        dall[g, 1, n] = jnp.where(lane < half, top, total)
    for i in range(1, groups):
        da_copy(i).start()

    lax.fori_loop(cut, far, far_step, 0)

    def finish(h, carry):
        a = acc[h]
        out_ref[:, pl.ds(pl.multiple_of(h * HD, HD), HD)] = (
            a[:, :HD] / a[:, HD:]).astype(out_ref.dtype)
        return carry

    lax.fori_loop(0, lh, finish, 0)

    for i in range(1, groups):
        da_copy(i).wait_recv()
    for r in range(served):
        mine = g * served + r

        def peak(e, top):
            for n in range(slots):
                m = jnp.broadcast_to(dall[e, 1, n][:, :1], (lh, HD))
                top = jnp.maximum(top, jnp.where(own_ref[e * slots + n] == mine, m, LOW))
            return top

        top = lax.fori_loop(0, groups, peak, jnp.full((lh, HD), LOW, jnp.float32))

        def gather(e, carry):
            num, den = carry
            for n in range(slots):
                x = dall[e, 1, n]
                hit = own_ref[e * slots + n] == mine
                f = jnp.where(hit, jnp.exp2(jnp.minimum(x[:, :1] - top, 0.0)), 0.0)
                num = num + f * dall[e, 0, n]
                den = den + f * x[:, half:half + 1]
            return num, den

        zero = jnp.zeros((lh, HD), jnp.float32)
        num, den = lax.fori_loop(0, groups, gather, (zero, zero))
        dout_ref[r] = (num / den).astype(dout_ref.dtype)

    for i in range(1, tp):
        dq1_copy(i).wait_send()
        dp_copy(i).wait_send()
    for i in range(1, groups):
        dq2_copy(i).wait_send()
        da_copy(i).wait_send()
    for s in range(1, tp):
        for p in range(pieces):
            kv_copy(s, p).wait_send()


def on_device(pf_query, pf_cache, pf_offset, dec_query, dec_cache, slot_owner, slot_len):
    tp = lax.axis_size("tp")
    groups = lax.axis_size("group")
    rows, llen = pf_query.shape[0], pf_cache.shape[2]
    lh = QH // tp
    kvl = max(1, lh // WIDTH)
    served, slots, slen = dec_query.shape[0], dec_cache.shape[0], dec_cache.shape[2]
    block = min(512, llen)
    pieces = llen // block
    cfg = (tp, groups, rows, llen, block, lh, kvl, served, slots, slen)
    dq = dec_query.reshape(served, lh, HD).astype(jnp.float32)
    dma = pltpu.SemaphoreType.DMA
    smem = pl.BlockSpec(memory_space=pltpu.SMEM)
    anywhere = pl.BlockSpec(memory_space=pl.ANY)
    vmem = pl.BlockSpec(memory_space=pltpu.VMEM)
    pf_out, dec_out = pl.pallas_call(
        functools.partial(kernel, cfg),
        out_shape=(
            jax.ShapeDtypeStruct((rows, lh * HD), jnp.bfloat16),
            jax.ShapeDtypeStruct((served, lh, HD), jnp.bfloat16),
        ),
        in_specs=[smem, smem, smem, anywhere, anywhere, anywhere, anywhere],
        out_specs=(vmem, vmem),
        scratch_shapes=[
            pltpu.VMEM((rows, lh * HD), jnp.bfloat16),
            pltpu.VMEM((tp, 2, llen, kvl * HD), jnp.bfloat16),
            pltpu.VMEM(dec_cache.shape, jnp.bfloat16),
            pltpu.VMEM((rows, block), jnp.float32),
            pltpu.VMEM((lh, rows, 2 * HD), jnp.float32),
            pltpu.VMEM((lh, rows, HD), jnp.float32),
            pltpu.VMEM((groups, served, tp, lh, HD), jnp.float32),
            pltpu.VMEM((tp, 2, slots, lh, HD), jnp.float32),
            pltpu.VMEM((tp, 2, slots, lh, HD), jnp.float32),
            pltpu.VMEM((groups, 2, slots, lh, HD), jnp.float32),
            dma((3,)),
            dma((pieces,)),
            dma((tp, pieces)),
            dma((tp, pieces)),
            dma((tp,)),
            dma((tp,)),
            dma((groups,)),
            dma((groups,)),
            dma((tp,)),
            dma((tp,)),
            dma((groups,)),
            dma((groups,)),
        ],
        compiler_params=pltpu.CompilerParams(
            collective_id=0, has_side_effects=True, vmem_limit_bytes=48 * 1024 * 1024),
    )(pf_offset, slot_owner, slot_len, pf_query, pf_cache, dq, dec_cache)
    return pf_out, dec_out.reshape(served, lh * HD)


def solution(mesh):
    placed = (
        P("group", "tp"),
        P("group", None, "tp", None),
        P(),
        P("group", "tp"),
        P("group", None, "tp", None),
        P(),
        P(),
    )
    return jax.shard_map(
        on_device,
        mesh=mesh,
        in_specs=placed,
        out_specs=(P("group", "tp"), P("group", "tp")),
        check_vma=False,
    )
```

```python
import functools
import math
import jax
import jax.numpy as jnp
from jax import lax
from jax.experimental import pallas as pl
from jax.experimental.pallas import tpu as pltpu
from jax.sharding import PartitionSpec as P

QH = 64
KVH = 8
HD = 128
WIDTH = QH // KVH
LOW = -1e30
STACK = 2
EXTRA = 16
SCALE = HD ** (-0.5) * math.log2(math.e)


def kernel(cfg, off_hbm, own_hbm, len_hbm, q_hbm, kv_hbm, dq_hbm, dkv_hbm, out_ref, dout_ref,
           off_ref, own_ref, len_ref, q_ref, dq_ref, q2, kvbuf, dkv, vt, bias, acc, mrow, dqtp, dqbuf,
           dpart, dpeer, dall, loc_sem, own_sem, kv_send, kv_recv, dq1_send, dq1_recv, dq2_send, dq2_recv,
           dp_send, dp_recv, da_send, da_recv):
    tp, groups, rows, llen, block, stack, lh, kvl, served, slots, slen = cfg
    pieces = llen // block
    chips = tp // 2
    cols = kvl * HD
    t = lax.axis_index("tp")
    g = lax.axis_index("group")
    chip, core = t // 2, t % 2

    def source(s):
        return lax.rem(chip + s // 2, chips) * 2 + lax.rem(core + s % 2, 2)

    def target(s):
        return lax.rem(chip + chips - s // 2, chips) * 2 + lax.rem(core + s % 2, 2)

    def kv_copy(s, piece):
        dest = target(s)
        col = pl.multiple_of((dest * lh // WIDTH) * HD, HD)
        at = pl.ds(piece * block, block)
        return pltpu.make_async_remote_copy(
            src_ref=kv_hbm.at[0, :, at, pl.ds(col, cols)],
            dst_ref=kvbuf.at[s, :, at, :],
            send_sem=kv_send.at[s, piece],
            recv_sem=kv_recv.at[s, piece],
            device_id={"tp": dest},
            device_id_type=pl.DeviceIdType.MESH,
        )

    def own_copy(piece):
        col = pl.multiple_of((t * lh // WIDTH) * HD, HD)
        at = pl.ds(piece * block, block)
        return pltpu.make_async_copy(
            kv_hbm.at[0, :, at, pl.ds(col, cols)], kvbuf.at[0, :, at, :], own_sem.at[piece])

    def dq1_copy(i):
        return pltpu.make_async_remote_copy(
            src_ref=dqtp.at[t], dst_ref=dqtp.at[t], send_sem=dq1_send.at[i],
            recv_sem=dq1_recv.at[i], device_id={"tp": lax.rem(t + i, tp)},
            device_id_type=pl.DeviceIdType.MESH)

    def dq2_copy(i):
        return pltpu.make_async_remote_copy(
            src_ref=dqbuf.at[g], dst_ref=dqbuf.at[g], send_sem=dq2_send.at[i],
            recv_sem=dq2_recv.at[i], device_id={"group": lax.rem(g + i, groups)},
            device_id_type=pl.DeviceIdType.MESH)

    def dp_copy(i):
        dest = lax.rem(t + i, tp)
        return pltpu.make_async_remote_copy(
            src_ref=dpart.at[dest], dst_ref=dpeer.at[i], send_sem=dp_send.at[i],
            recv_sem=dp_recv.at[i], device_id={"tp": dest},
            device_id_type=pl.DeviceIdType.MESH)

    def da_copy(i):
        return pltpu.make_async_remote_copy(
            src_ref=dall.at[g], dst_ref=dall.at[g], send_sem=da_send.at[i],
            recv_sem=da_recv.at[i], device_id={"group": lax.rem(g + i, groups)},
            device_id_type=pl.DeviceIdType.MESH)

    q_copy = pltpu.make_async_copy(q_hbm, q_ref, loc_sem.at[0])
    dq0_copy = pltpu.make_async_copy(dq_hbm, dq_ref, loc_sem.at[1])
    ints = [pltpu.make_async_copy(src, dst, loc_sem.at[3 + i]) for i, (src, dst) in enumerate(
        ((off_hbm, off_ref), (own_hbm, own_ref), (len_hbm, len_ref)))]
    dkv_copy = pltpu.make_async_copy(dkv_hbm, dkv, loc_sem.at[2])
    dq0_copy.start()
    q_copy.start()
    for copy in ints:
        copy.start()
    for p in range(pieces):
        own_copy(p).start()

    barrier = pltpu.get_barrier_semaphore()
    for i in range(1, tp):
        pl.semaphore_signal(barrier, inc=1, device_id={"tp": lax.rem(t + i, tp)},
                            device_id_type=pl.DeviceIdType.MESH)
    for i in range(1, groups):
        pl.semaphore_signal(barrier, inc=1, device_id={"group": lax.rem(g + i, groups)},
                            device_id_type=pl.DeviceIdType.MESH)
    dq0_copy.wait()
    for r in range(served):
        for h in range(lh):
            dqtp[t, r, h:h + 1, :] = dq_ref[r:r + 1, h * HD:(h + 1) * HD].astype(jnp.float32)
    pl.semaphore_wait(barrier, tp - 1 + groups - 1)

    for i in range(1, tp):
        dq1_copy(i).start()
    early = [(2 * j + i, p) for j in range(1, chips) for p in range(pieces) for i in range(2)]
    cut = (chips - 1) * pieces // 2
    early, late = early[:2 * cut], early[2 * cut:]
    for s, p in early:
        kv_copy(s, p).start()
    for p in range(pieces):
        kv_copy(1, p).start()
    dkv_copy.start()
    acc[...] = jnp.zeros_like(acc)
    mrow[...] = jnp.full_like(mrow, LOW)
    for copy in ints:
        copy.wait()
    offset = off_ref[g]
    q_copy.wait()

    def split(b, carry):
        for e in range(stack):
            at = pl.ds(pl.multiple_of((b * stack + e) * HD, HD), HD)
            q = q_ref[:, at].astype(jnp.float32).T * SCALE
            high = q.astype(jnp.bfloat16)
            q2[b, :HD, e * rows:(e + 1) * rows] = high
            q2[b, HD:, e * rows:(e + 1) * rows] = (
                q - high.astype(jnp.float32)).astype(jnp.bfloat16)
        return carry

    lax.fori_loop(0, lh // stack, split, 0)
    vt[:, HD:, :] = jnp.ones((kvl, EXTRA, vt.shape[2]), jnp.bfloat16)

    def attend(parts, length):
        for e, (s, start) in enumerate(parts):
            at = pl.ds(e * length, length)
            pos = lax.broadcasted_iota(jnp.int32, (length, rows), 0) + (source(s) * llen + start)
            tok = lax.broadcasted_iota(jnp.int32, (length, rows), 1) + offset
            bias[at, :] = jnp.where(pos <= tok, 0.0, LOW)
            for k in range(kvl):
                vt[k, :HD, at] = kvbuf[s, 1, pl.ds(start, length), k * HD:(k + 1) * HD].T

        def some(b, carry):
            kv = b * stack // WIDTH
            kcol = pl.ds(pl.multiple_of(kv * HD, HD), HD)
            q = q2[b]
            old = mrow[b, :1, :]
            previous = acc[b]
            top = old
            scores = []
            for e, (s, start) in enumerate(parts):
                k = kvbuf[s, 0, pl.ds(start, length), kcol]
                sc = jnp.dot(jnp.concatenate([k, k], axis=1), q,
                             preferred_element_type=jnp.float32)
                mask = bias[pl.ds(e * length, length), :]
                sc = sc + jnp.concatenate([mask] * stack, axis=1)
                top = jnp.maximum(top, jnp.max(sc, axis=0, keepdims=True))
                scores.append(sc)
            out = previous * jnp.exp2(old - top)
            for e, sc in enumerate(scores):
                w = jnp.exp2(sc - top).astype(jnp.bfloat16)
                out += jnp.dot(vt[kv, :, pl.ds(e * length, length)], w,
                               preferred_element_type=jnp.float32)
            mrow[b] = jnp.broadcast_to(top, mrow.shape[1:])
            acc[b] = out
            return carry

        lax.fori_loop(0, lh // stack, some, 0)

    def far_step(b, carry):
        j, p = 1 + b // pieces, b % pieces
        for i in range(2):
            kv_copy(2 * j + i, p).wait_recv()
        start = pl.multiple_of(p * block, block)
        attend([(2 * j, start), (2 * j + 1, start)], block)
        return carry

    for p in range(pieces):
        own_copy(p).wait()
    attend([(0, p * block) for p in range(pieces)], block)

    for i in range(1, tp):
        dq1_copy(i).wait_recv()
    for r in range(served):
        whole = jnp.concatenate([dqtp[e, r] for e in range(tp)], axis=0)
        dqbuf[g, r] = whole.astype(jnp.bfloat16)
    for i in range(1, groups):
        dq2_copy(i).start()

    for p in range(pieces):
        kv_copy(1, p).wait_recv()
    attend([(1, p * block) for p in range(pieces)], block)

    dkv_copy.wait()
    for i in range(1, groups):
        dq2_copy(i).wait_recv()
    span = HD // slots
    lane = lax.broadcasted_iota(jnp.int32, (QH, HD), 1)
    stat = jnp.zeros((QH, HD), jnp.float32)
    for n in range(slots):
        owner = own_ref[g * slots + n]
        query = dqbuf[owner // served, owner % served].astype(jnp.float32)
        wide = jnp.concatenate([query.T] * KVH, axis=0)
        r = lax.broadcasted_iota(jnp.int32, (KVH * HD, QH), 0) // HD
        c = lax.broadcasted_iota(jnp.int32, (KVH * HD, QH), 1) // WIDTH
        wide = jnp.where(r == c, wide, 0.0).astype(jnp.bfloat16)
        sc = jnp.dot(dkv[n, 0], wide, preferred_element_type=jnp.float32).T
        pos = lax.broadcasted_iota(jnp.int32, (QH, slen), 1) + t * slen
        live = pos < len_ref[g * slots + n]
        sc = jnp.where(live, sc * SCALE, LOW)
        top = jnp.max(sc, axis=1, keepdims=True)
        w = jnp.where(live, jnp.exp2(sc - top), 0.0).astype(jnp.bfloat16)
        total = jnp.sum(w.astype(jnp.float32), axis=1, keepdims=True)
        o = jnp.dot(w, dkv[n, 1], preferred_element_type=jnp.float32)
        o = jnp.concatenate(
            [o[k * WIDTH:(k + 1) * WIDTH, k * HD:(k + 1) * HD] for k in range(KVH)], axis=0)
        stat = jnp.where(lane == n * span, top, stat)
        stat = jnp.where(lane == n * span + 1, total, stat)
        for d in range(tp):
            dpart[d, n] = o[d * lh:(d + 1) * lh]
    for d in range(tp):
        dpart[d, slots] = stat[d * lh:(d + 1) * lh]
    for i in range(1, tp):
        dp_copy(i).start()
    for s, p in late:
        kv_copy(s, p).start()

    far = (chips - 1) * pieces
    lax.fori_loop(0, cut, far_step, 0)

    for i in range(1, tp):
        dp_copy(i).wait_recv()
    lane = lax.broadcasted_iota(jnp.int32, (lh, HD), 1)
    joined = jnp.zeros((lh, HD), jnp.float32)
    stats = [dpart[t, slots]] + [dpeer[i, slots] for i in range(1, tp)]
    for n in range(slots):
        accs = [dpart[t, n]] + [dpeer[i, n] for i in range(1, tp)]
        at = n * span
        top = functools.reduce(jnp.maximum, [x[:, at:at + 1] for x in stats])
        fac = [jnp.exp2(x[:, at:at + 1] - top) for x in stats]
        total = sum(f * x[:, at + 1:at + 2] for f, x in zip(fac, stats))
        dall[g, n] = sum(f * a for f, a in zip(fac, accs))
        joined = jnp.where(lane == at, top, joined)
        joined = jnp.where(lane == at + 1, total, joined)
    dall[g, slots] = joined
    for i in range(1, groups):
        da_copy(i).start()

    lax.fori_loop(cut, far, far_step, 0)

    def finish(b, carry):
        a = acc[b]
        a = a[:HD] / a[HD:HD + 1]
        for e in range(stack):
            at = pl.ds(pl.multiple_of((b * stack + e) * HD, HD), HD)
            out_ref[:, at] = a[:, e * rows:(e + 1) * rows].T.astype(out_ref.dtype)
        return carry

    lax.fori_loop(0, lh // stack, finish, 0)

    for i in range(1, groups):
        da_copy(i).wait_recv()
    for r in range(served):
        mine = g * served + r

        def peak(e, top):
            for n in range(slots):
                m = jnp.broadcast_to(dall[e, slots][:, n * span:n * span + 1], (lh, HD))
                top = jnp.maximum(top, jnp.where(own_ref[e * slots + n] == mine, m, LOW))
            return top

        top = lax.fori_loop(0, groups, peak, jnp.full((lh, HD), LOW, jnp.float32))

        def gather(e, carry):
            num, den = carry
            for n in range(slots):
                x = dall[e, slots][:, n * span:n * span + 2]
                hit = own_ref[e * slots + n] == mine
                f = jnp.where(hit, jnp.exp2(jnp.minimum(x[:, :1] - top, 0.0)), 0.0)
                num = num + f * dall[e, n]
                den = den + f * x[:, 1:2]
            return num, den

        zero = jnp.zeros((lh, HD), jnp.float32)
        num, den = lax.fori_loop(0, groups, gather, (zero, zero))
        res = num / den
        for h in range(lh):
            dout_ref[r:r + 1, h * HD:(h + 1) * HD] = res[h:h + 1].astype(dout_ref.dtype)

    for i in range(1, tp):
        dq1_copy(i).wait_send()
        dp_copy(i).wait_send()
    for i in range(1, groups):
        dq2_copy(i).wait_send()
        da_copy(i).wait_send()
    for s in range(1, tp):
        for p in range(pieces):
            kv_copy(s, p).wait_send()


def on_device(pf_query, pf_cache, pf_offset, dec_query, dec_cache, slot_owner, slot_len):
    tp = lax.axis_size("tp")
    groups = lax.axis_size("group")
    rows, llen = pf_query.shape[0], pf_cache.shape[2]
    lh = QH // tp
    kvl = max(1, lh // WIDTH)
    served, slots, slen = dec_query.shape[0], dec_cache.shape[0], dec_cache.shape[2]
    block = min(512, llen)
    pieces = llen // block
    span = max(2 * block, llen)
    cfg = (tp, groups, rows, llen, block, STACK, lh, kvl, served, slots, slen)
    dma = pltpu.SemaphoreType.DMA
    anywhere = pl.BlockSpec(memory_space=pl.ANY)
    vmem = pl.BlockSpec(memory_space=pltpu.VMEM)
    pf_out, dec_out = pl.pallas_call(
        functools.partial(kernel, cfg),
        out_shape=(
            jax.ShapeDtypeStruct((rows, lh * HD), jnp.bfloat16),
            jax.ShapeDtypeStruct((served, lh * HD), jnp.bfloat16),
        ),
        in_specs=[anywhere] * 7,
        out_specs=(vmem, vmem),
        scratch_shapes=[
            pltpu.SMEM(pf_offset.shape, jnp.int32),
            pltpu.SMEM(slot_owner.shape, jnp.int32),
            pltpu.SMEM(slot_len.shape, jnp.int32),
            pltpu.VMEM((rows, lh * HD), jnp.bfloat16),
            pltpu.VMEM((served, lh * HD), jnp.bfloat16),
            pltpu.VMEM((lh // STACK, 2 * HD, STACK * rows), jnp.bfloat16),
            pltpu.VMEM((tp, 2, llen, kvl * HD), jnp.bfloat16),
            pltpu.VMEM(dec_cache.shape, jnp.bfloat16),
            pltpu.VMEM((kvl, HD + EXTRA, span), jnp.bfloat16),
            pltpu.VMEM((span, rows), jnp.float32),
            pltpu.VMEM((lh // STACK, HD + EXTRA, STACK * rows), jnp.float32),
            pltpu.VMEM((lh // STACK, 8, STACK * rows), jnp.float32),
            pltpu.VMEM((tp, served, lh, HD), jnp.float32),
            pltpu.VMEM((groups, served, QH, HD), jnp.bfloat16),
            pltpu.VMEM((tp, slots + 1, lh, HD), jnp.float32),
            pltpu.VMEM((tp, slots + 1, lh, HD), jnp.float32),
            pltpu.VMEM((groups, slots + 1, lh, HD), jnp.float32),
            dma((6,)),
            dma((pieces,)),
            dma((tp, pieces)),
            dma((tp, pieces)),
            dma((tp,)),
            dma((tp,)),
            dma((groups,)),
            dma((groups,)),
            dma((tp,)),
            dma((tp,)),
            dma((groups,)),
            dma((groups,)),
        ],
        compiler_params=pltpu.CompilerParams(
            collective_id=0, has_side_effects=True, vmem_limit_bytes=60 * 1024 * 1024),
    )(pf_offset, slot_owner, slot_len, pf_query, pf_cache, dec_query, dec_cache)
    return pf_out, dec_out


def solution(mesh):
    placed = (
        P("group", "tp"),
        P("group", None, "tp", None),
        P(),
        P("group", "tp"),
        P("group", None, "tp", None),
        P(),
        P(),
    )
    return jax.shard_map(
        on_device,
        mesh=mesh,
        in_specs=placed,
        out_specs=(P("group", "tp"), P("group", "tp")),
        check_vma=False,
    )
```

```python
import functools
import math
import jax
import jax.numpy as jnp
from jax import lax
from jax.experimental import pallas as pl
from jax.experimental.pallas import tpu as pltpu
from jax.sharding import PartitionSpec as P

QH = 64
KVH = 8
HD = 128
WIDTH = QH // KVH
LOW = -1e30
STACK = 4
EXTRA = 16
SCALE = HD ** (-0.5) * math.log2(math.e)


def kernel(cfg, off_hbm, own_hbm, len_hbm, q_hbm, kv_hbm, dq_hbm, dkv_hbm, out_ref, dout_ref,
           off_ref, own_ref, len_ref, q_ref, dq_ref, q2, kvbuf, dkv, vt, bias, acc, mrow, dqtp, dqbuf,
           dpart, dpeer, dall, loc_sem, own_sem, kv_send, kv_recv, dq1_send, dq1_recv, dq2_send, dq2_recv,
           dp_send, dp_recv, da_send, da_recv):
    tp, groups, rows, llen, block, stack, lh, kvl, served, slots, slen = cfg
    pieces = llen // block
    chips = tp // 2
    cols = kvl * HD
    t = lax.axis_index("tp")
    g = lax.axis_index("group")
    chip, core = t // 2, t % 2

    def source(s):
        return lax.rem(chip + s // 2, chips) * 2 + lax.rem(core + s % 2, 2)

    def target(s):
        return lax.rem(chip + chips - s // 2, chips) * 2 + lax.rem(core + s % 2, 2)

    def kv_copy(s, piece):
        dest = target(s)
        col = pl.multiple_of((dest * lh // WIDTH) * HD, HD)
        at = pl.ds(piece * block, block)
        return pltpu.make_async_remote_copy(
            src_ref=kv_hbm.at[0, :, at, pl.ds(col, cols)],
            dst_ref=kvbuf.at[s, :, at, :],
            send_sem=kv_send.at[s, piece],
            recv_sem=kv_recv.at[s, piece],
            device_id={"tp": dest},
            device_id_type=pl.DeviceIdType.MESH,
        )

    def own_copy(piece):
        col = pl.multiple_of((t * lh // WIDTH) * HD, HD)
        at = pl.ds(piece * block, block)
        return pltpu.make_async_copy(
            kv_hbm.at[0, :, at, pl.ds(col, cols)], kvbuf.at[0, :, at, :], own_sem.at[piece])

    def dq1_copy(i):
        return pltpu.make_async_remote_copy(
            src_ref=dqtp.at[t], dst_ref=dqtp.at[t], send_sem=dq1_send.at[i],
            recv_sem=dq1_recv.at[i], device_id={"tp": lax.rem(t + i, tp)},
            device_id_type=pl.DeviceIdType.MESH)

    def dq2_copy(i):
        return pltpu.make_async_remote_copy(
            src_ref=dqbuf.at[g], dst_ref=dqbuf.at[g], send_sem=dq2_send.at[i],
            recv_sem=dq2_recv.at[i], device_id={"group": lax.rem(g + i, groups)},
            device_id_type=pl.DeviceIdType.MESH)

    def dp_copy(i):
        dest = lax.rem(t + i, tp)
        return pltpu.make_async_remote_copy(
            src_ref=dpart.at[dest], dst_ref=dpeer.at[i], send_sem=dp_send.at[i],
            recv_sem=dp_recv.at[i], device_id={"tp": dest},
            device_id_type=pl.DeviceIdType.MESH)

    def da_copy(i):
        return pltpu.make_async_remote_copy(
            src_ref=dall.at[g], dst_ref=dall.at[g], send_sem=da_send.at[i],
            recv_sem=da_recv.at[i], device_id={"group": lax.rem(g + i, groups)},
            device_id_type=pl.DeviceIdType.MESH)

    q_copy = pltpu.make_async_copy(q_hbm, q_ref, loc_sem.at[0])
    dq0_copy = pltpu.make_async_copy(dq_hbm, dq_ref, loc_sem.at[1])
    ints = [pltpu.make_async_copy(src, dst, loc_sem.at[3 + i]) for i, (src, dst) in enumerate(
        ((off_hbm, off_ref), (own_hbm, own_ref), (len_hbm, len_ref)))]
    dkv_copy = pltpu.make_async_copy(dkv_hbm, dkv, loc_sem.at[2])
    dq0_copy.start()
    q_copy.start()
    for copy in ints:
        copy.start()
    for p in range(pieces):
        own_copy(p).start()

    barrier = pltpu.get_barrier_semaphore()
    for i in range(1, tp):
        pl.semaphore_signal(barrier, inc=1, device_id={"tp": lax.rem(t + i, tp)},
                            device_id_type=pl.DeviceIdType.MESH)
    for i in range(1, groups):
        pl.semaphore_signal(barrier, inc=1, device_id={"group": lax.rem(g + i, groups)},
                            device_id_type=pl.DeviceIdType.MESH)
    dq0_copy.wait()
    for r in range(served):
        for h in range(lh):
            dqtp[t, r, h:h + 1, :] = dq_ref[r:r + 1, h * HD:(h + 1) * HD].astype(jnp.float32)
    pl.semaphore_wait(barrier, tp - 1 + groups - 1)

    for i in range(1, tp):
        dq1_copy(i).start()
    early = [(2 * j + i, p) for j in range(1, chips) for p in range(pieces) for i in range(2)]
    cut = (chips - 1) * pieces // 2
    early, late = early[:2 * cut], early[2 * cut:]
    for s, p in early:
        kv_copy(s, p).start()
    for p in range(pieces):
        kv_copy(1, p).start()
    dkv_copy.start()
    acc[...] = jnp.zeros_like(acc)
    mrow[...] = jnp.full_like(mrow, LOW)
    for copy in ints:
        copy.wait()
    offset = off_ref[g]
    q_copy.wait()

    def split(b, carry):
        for e in range(stack):
            at = pl.ds(pl.multiple_of((b * stack + e) * HD, HD), HD)
            q = q_ref[:, at].astype(jnp.float32).T * SCALE
            high = q.astype(jnp.bfloat16)
            q2[b, :HD, e * rows:(e + 1) * rows] = high
            q2[b, HD:, e * rows:(e + 1) * rows] = (
                q - high.astype(jnp.float32)).astype(jnp.bfloat16)
        return carry

    lax.fori_loop(0, lh // stack, split, 0)
    vt[:, HD:, :] = jnp.ones((kvl, EXTRA, vt.shape[2]), jnp.bfloat16)

    def attend(parts, length):
        for e, (s, start) in enumerate(parts):
            at = pl.ds(e * length, length)
            pos = lax.broadcasted_iota(jnp.int32, (length, rows), 0) + (source(s) * llen + start)
            tok = lax.broadcasted_iota(jnp.int32, (length, rows), 1) + offset
            bias[at, :] = jnp.where(pos <= tok, 0.0, LOW)
            for k in range(kvl):
                vt[k, :HD, at] = kvbuf[s, 1, pl.ds(start, length), k * HD:(k + 1) * HD].T

        def some(b, carry):
            kv = b * stack // WIDTH
            kcol = pl.ds(pl.multiple_of(kv * HD, HD), HD)
            q = q2[b]
            old = mrow[b, :1, :]
            previous = acc[b]
            top = old
            scores = []
            for e, (s, start) in enumerate(parts):
                k = kvbuf[s, 0, pl.ds(start, length), kcol]
                sc = jnp.dot(jnp.concatenate([k, k], axis=1), q,
                             preferred_element_type=jnp.float32)
                mask = bias[pl.ds(e * length, length), :]
                sc = sc + jnp.concatenate([mask] * stack, axis=1)
                top = jnp.maximum(top, jnp.max(sc, axis=0, keepdims=True))
                scores.append(sc)
            out = previous * jnp.exp2(old - top)
            for e, sc in enumerate(scores):
                w = jnp.exp2(sc - top).astype(jnp.bfloat16)
                out += jnp.dot(vt[kv, :, pl.ds(e * length, length)], w,
                               preferred_element_type=jnp.float32)
            mrow[b] = jnp.broadcast_to(top, mrow.shape[1:])
            acc[b] = out
            return carry

        lax.fori_loop(0, lh // stack, some, 0)

    def far_step(b, carry):
        j, p = 1 + b // pieces, b % pieces
        for i in range(2):
            kv_copy(2 * j + i, p).wait_recv()
        start = pl.multiple_of(p * block, block)
        attend([(2 * j, start), (2 * j + 1, start)], block)
        return carry

    for p in range(pieces):
        own_copy(p).wait()
    attend([(0, p * block) for p in range(pieces)], block)

    for i in range(1, tp):
        dq1_copy(i).wait_recv()
    for r in range(served):
        whole = jnp.concatenate([dqtp[e, r] for e in range(tp)], axis=0)
        dqbuf[g, r] = whole.astype(jnp.bfloat16)
    for i in range(1, groups):
        dq2_copy(i).start()

    for p in range(pieces):
        kv_copy(1, p).wait_recv()
    attend([(1, p * block) for p in range(pieces)], block)

    dkv_copy.wait()
    for i in range(1, groups):
        dq2_copy(i).wait_recv()
    span = HD // slots
    lane = lax.broadcasted_iota(jnp.int32, (QH, HD), 1)
    stat = jnp.zeros((QH, HD), jnp.float32)
    for n in range(slots):
        owner = own_ref[g * slots + n]
        query = dqbuf[owner // served, owner % served].astype(jnp.float32)
        wide = jnp.concatenate([query.T] * KVH, axis=0)
        r = lax.broadcasted_iota(jnp.int32, (KVH * HD, QH), 0) // HD
        c = lax.broadcasted_iota(jnp.int32, (KVH * HD, QH), 1) // WIDTH
        wide = jnp.where(r == c, wide, 0.0).astype(jnp.bfloat16)
        sc = jnp.dot(dkv[n, 0], wide, preferred_element_type=jnp.float32).T
        pos = lax.broadcasted_iota(jnp.int32, (QH, slen), 1) + t * slen
        live = pos < len_ref[g * slots + n]
        sc = jnp.where(live, sc * SCALE, LOW)
        top = jnp.max(sc, axis=1, keepdims=True)
        w = jnp.where(live, jnp.exp2(sc - top), 0.0).astype(jnp.bfloat16)
        total = jnp.sum(w.astype(jnp.float32), axis=1, keepdims=True)
        o = jnp.dot(w, dkv[n, 1], preferred_element_type=jnp.float32)
        o = jnp.concatenate(
            [o[k * WIDTH:(k + 1) * WIDTH, k * HD:(k + 1) * HD] for k in range(KVH)], axis=0)
        stat = jnp.where(lane == n * span, top, stat)
        stat = jnp.where(lane == n * span + 1, total, stat)
        for d in range(tp):
            dpart[d, n] = o[d * lh:(d + 1) * lh]
    for d in range(tp):
        dpart[d, slots] = stat[d * lh:(d + 1) * lh]
    for i in range(1, tp):
        dp_copy(i).start()
    for s, p in late:
        kv_copy(s, p).start()

    far = (chips - 1) * pieces
    lax.fori_loop(0, cut, far_step, 0)

    for i in range(1, tp):
        dp_copy(i).wait_recv()
    lane = lax.broadcasted_iota(jnp.int32, (lh, HD), 1)
    joined = jnp.zeros((lh, HD), jnp.float32)
    stats = [dpart[t, slots]] + [dpeer[i, slots] for i in range(1, tp)]
    for n in range(slots):
        accs = [dpart[t, n]] + [dpeer[i, n] for i in range(1, tp)]
        at = n * span
        top = functools.reduce(jnp.maximum, [x[:, at:at + 1] for x in stats])
        fac = [jnp.exp2(x[:, at:at + 1] - top) for x in stats]
        total = sum(f * x[:, at + 1:at + 2] for f, x in zip(fac, stats))
        dall[g, n] = sum(f * a for f, a in zip(fac, accs))
        joined = jnp.where(lane == at, top, joined)
        joined = jnp.where(lane == at + 1, total, joined)
    dall[g, slots] = joined
    for i in range(1, groups):
        da_copy(i).start()

    lax.fori_loop(cut, far, far_step, 0)

    def finish(b, carry):
        a = acc[b]
        a = a[:HD] / a[HD:HD + 1]
        for e in range(stack):
            at = pl.ds(pl.multiple_of((b * stack + e) * HD, HD), HD)
            out_ref[:, at] = a[:, e * rows:(e + 1) * rows].T.astype(out_ref.dtype)
        return carry

    lax.fori_loop(0, lh // stack, finish, 0)

    for i in range(1, groups):
        da_copy(i).wait_recv()
    for r in range(served):
        mine = g * served + r

        def peak(e, top):
            for n in range(slots):
                m = jnp.broadcast_to(dall[e, slots][:, n * span:n * span + 1], (lh, HD))
                top = jnp.maximum(top, jnp.where(own_ref[e * slots + n] == mine, m, LOW))
            return top

        top = lax.fori_loop(0, groups, peak, jnp.full((lh, HD), LOW, jnp.float32))

        def gather(e, carry):
            num, den = carry
            for n in range(slots):
                x = dall[e, slots][:, n * span:n * span + 2]
                hit = own_ref[e * slots + n] == mine
                f = jnp.where(hit, jnp.exp2(jnp.minimum(x[:, :1] - top, 0.0)), 0.0)
                num = num + f * dall[e, n]
                den = den + f * x[:, 1:2]
            return num, den

        zero = jnp.zeros((lh, HD), jnp.float32)
        num, den = lax.fori_loop(0, groups, gather, (zero, zero))
        res = num / den
        for h in range(lh):
            dout_ref[r:r + 1, h * HD:(h + 1) * HD] = res[h:h + 1].astype(dout_ref.dtype)

    for i in range(1, tp):
        dq1_copy(i).wait_send()
        dp_copy(i).wait_send()
    for i in range(1, groups):
        dq2_copy(i).wait_send()
        da_copy(i).wait_send()
    for s in range(1, tp):
        for p in range(pieces):
            kv_copy(s, p).wait_send()


def on_device(pf_query, pf_cache, pf_offset, dec_query, dec_cache, slot_owner, slot_len):
    tp = lax.axis_size("tp")
    groups = lax.axis_size("group")
    rows, llen = pf_query.shape[0], pf_cache.shape[2]
    lh = QH // tp
    kvl = max(1, lh // WIDTH)
    served, slots, slen = dec_query.shape[0], dec_cache.shape[0], dec_cache.shape[2]
    block = min(256, llen)
    pieces = llen // block
    span = max(2 * block, llen)
    cfg = (tp, groups, rows, llen, block, STACK, lh, kvl, served, slots, slen)
    dma = pltpu.SemaphoreType.DMA
    anywhere = pl.BlockSpec(memory_space=pl.ANY)
    vmem = pl.BlockSpec(memory_space=pltpu.VMEM)
    pf_out, dec_out = pl.pallas_call(
        functools.partial(kernel, cfg),
        out_shape=(
            jax.ShapeDtypeStruct((rows, lh * HD), jnp.bfloat16),
            jax.ShapeDtypeStruct((served, lh * HD), jnp.bfloat16),
        ),
        in_specs=[anywhere] * 7,
        out_specs=(vmem, vmem),
        scratch_shapes=[
            pltpu.SMEM(pf_offset.shape, jnp.int32),
            pltpu.SMEM(slot_owner.shape, jnp.int32),
            pltpu.SMEM(slot_len.shape, jnp.int32),
            pltpu.VMEM((rows, lh * HD), jnp.bfloat16),
            pltpu.VMEM((served, lh * HD), jnp.bfloat16),
            pltpu.VMEM((lh // STACK, 2 * HD, STACK * rows), jnp.bfloat16),
            pltpu.VMEM((tp, 2, llen, kvl * HD), jnp.bfloat16),
            pltpu.VMEM(dec_cache.shape, jnp.bfloat16),
            pltpu.VMEM((kvl, HD + EXTRA, span), jnp.bfloat16),
            pltpu.VMEM((span, rows), jnp.float32),
            pltpu.VMEM((lh // STACK, HD + EXTRA, STACK * rows), jnp.float32),
            pltpu.VMEM((lh // STACK, 8, STACK * rows), jnp.float32),
            pltpu.VMEM((tp, served, lh, HD), jnp.float32),
            pltpu.VMEM((groups, served, QH, HD), jnp.bfloat16),
            pltpu.VMEM((tp, slots + 1, lh, HD), jnp.float32),
            pltpu.VMEM((tp, slots + 1, lh, HD), jnp.float32),
            pltpu.VMEM((groups, slots + 1, lh, HD), jnp.float32),
            dma((6,)),
            dma((pieces,)),
            dma((tp, pieces)),
            dma((tp, pieces)),
            dma((tp,)),
            dma((tp,)),
            dma((groups,)),
            dma((groups,)),
            dma((tp,)),
            dma((tp,)),
            dma((groups,)),
            dma((groups,)),
        ],
        compiler_params=pltpu.CompilerParams(
            collective_id=0, has_side_effects=True, vmem_limit_bytes=60 * 1024 * 1024),
    )(pf_offset, slot_owner, slot_len, pf_query, pf_cache, dec_query, dec_cache)
    return pf_out, dec_out


def solution(mesh):
    placed = (
        P("group", "tp"),
        P("group", None, "tp", None),
        P(),
        P("group", "tp"),
        P("group", None, "tp", None),
        P(),
        P(),
    )
    return jax.shard_map(
        on_device,
        mesh=mesh,
        in_specs=placed,
        out_specs=(P("group", "tp"), P("group", "tp")),
        check_vma=False,
    )
```
